128 devices in a mesh: replica: 2 (over z_lo), fsdp: 64 (over x, y, z_hi, core).
Axes of the slice: x: 4, y: 4, z: 4 (z_hi: 2, z_lo: 2; z = z_hi * 2 + z_lo), core: 2. Of those that a mesh axis runs over, the one named last changes fastest.
Arguments:
- inputs: bfloat16 [2, 2, 65536, 4096], P('replica', None, 'fsdp'), may hold values from -16 to 16
- targets: bfloat16 [2, 2, 65536, 512], P('replica', None, 'fsdp'), may hold values from -6 to 6
- weights: float32 [2, 4096, 512], P('replica', 'fsdp'), may hold values from -6 to 6
- first_moment: float32 [2, 4096, 512], P('replica', 'fsdp'), may hold values from -18 to 18
- second_moment: float32 [2, 4096, 512], P('replica', 'fsdp'), may hold values from 4 to 100
- global_weights: float32 [4096, 512], P('fsdp'), may hold values from -6 to 6
- outer_momentum: float32 [4096, 512], P('fsdp'), may hold values from -2 to 2
- outer_gradient: bfloat16 [2, 4096, 512], P('replica', 'fsdp'), may hold values from -2 to 2
- sync_step: int32 [1], replicated, may hold values from 0 to 1
Outputs:
- weights_out: float32 [2, 4096, 512], P('replica', 'fsdp')
- first_out: float32 [2, 4096, 512], P('replica', 'fsdp')
- second_out: float32 [2, 4096, 512], P('replica', 'fsdp')
- global_out: float32 [4096, 512], P('fsdp')
- momentum_out: float32 [4096, 512], P('fsdp')
The draws below stay inside these ranges and needn't reach their ends.
Inputs may be any that keep to these rules, and one draw needn't show every extreme that they name: `sync_step`: the inner step after which each replica mixes in the new global weights; the same for both replicas.
All inputs are finite; a program needn't handle non-finite values.
Results may differ from the reference program's by a relative error of at most 0.008.
Values may be sent and summed in bfloat16 or wider, within the bound.
A program may use at most 256 MiB of HBM per device.

```python
import math
import jax
import jax.numpy as jnp
from jax import lax

D = 4096
KVW = 512
STEPS = 2
TOKENS = 65536
N_REPLICA = 2


def raised(array, stream_key, source, target, parts, factor):
    def block_of(axis_at):
        return (jnp.arange(array.shape[axis_at]) // (array.shape[axis_at] // parts)).reshape((-1,) + (1,) * (array.ndim - 1 - axis_at))

    first = jax.random.permutation(stream_key, parts)[block_of(target)]
    other_side = (block_of(target) + parts // 2) % parts
    return jnp.where((block_of(source) == first) | (block_of(source) == other_side), factor * array, array)


def shard_levels(own_key, shape, shards, least, high):
    def one(position, shards_of):
        heights = jax.random.uniform(jax.random.fold_in(jax.random.fold_in(own_key, 6), position), (shards_of,), jnp.float32, least / len(shards), high / len(shards))
        return jnp.repeat(jnp.exp(heights), shape[position] // shards_of).reshape((-1,) + (1,) * (len(shape) - position - 1))

    loudness = one(*shards[0])
    for cut in shards[1:]:
        loudness = loudness * one(*cut)
    return loudness


def noise(stream_key, shape, scale, bound, shards=(), kind=jnp.bfloat16):
    array = scale * jax.random.normal(stream_key, shape, jnp.float32)
    if shards:
        array = array * shard_levels(stream_key, shape, shards, -0.22, 0.18)
    return jnp.clip(array, -bound, bound).astype(kind)


def noise_with(key, shape, spread, reach, shards, heavy, dtype=jnp.bfloat16):
    drawn = spread * jax.random.normal(key, shape, jnp.float32)
    if shards:
        drawn = drawn * shard_levels(key, shape, shards, -0.22, 0.18)
    return jnp.clip(raised(drawn, jax.random.fold_in(key, 3), *heavy), -reach, reach).astype(dtype)


def setup_inputs(seed: int = 0) -> dict:
    splits = jax.random.split(jax.random.key(seed), 10)
    inputs = noise_with(splits[0], (N_REPLICA, STEPS, TOKENS, D), 1.0, 16.0, ((0, 2), (2, 64)), (2, 3, 64, 4.0))
    targets = noise(splits[1], (N_REPLICA, STEPS, TOKENS, KVW), 1.0, 6.0, ((0, 2), (2, 64)))
    weights = noise(splits[2], (N_REPLICA, D, KVW), 1.0, 6.0, ((0, 2), (1, 64)), jnp.float32)
    first_moment = noise(splits[3], (N_REPLICA, D, KVW), 3.0, 18.0, ((0, 2), (1, 64)), jnp.float32)
    second_moment = jnp.clip(jnp.exp(math.log(100.0) - 3.218876 * jax.random.uniform(splits[4], (N_REPLICA, D, KVW), jnp.float32) ** shard_levels(splits[4], (N_REPLICA, D, KVW), ((0, 2), (1, 64)), -0.2, 0.2)), 4.0, 100.0)
    global_weights = noise(splits[5], (D, KVW), 1.0, 6.0, ((0, 64),), jnp.float32)
    outer_momentum = noise(splits[6], (D, KVW), 0.3, 2.0, ((0, 64),), jnp.float32)
    outer_gradient = noise(splits[7], (N_REPLICA, D, KVW), 0.3, 2.0, ((0, 2), (1, 64)))
    sync_step = jax.random.randint(splits[8], (1,), 0, STEPS).astype(jnp.int32)
    return dict(inputs=inputs, targets=targets, weights=weights, first_moment=first_moment, second_moment=second_moment, global_weights=global_weights, outer_momentum=outer_momentum, outer_gradient=outer_gradient, sync_step=sync_step)


def reference(inputs, targets, weights, first_moment, second_moment, global_weights, outer_momentum, outer_gradient, sync_step):
    inv_root = 1.0 / math.sqrt(D)
    mean_change = lax.optimization_barrier(jnp.sum(outer_gradient.astype(jnp.float32), axis=0)) / N_REPLICA
    momentum_out = 0.9 * outer_momentum + mean_change
    global_out = global_weights - 0.7 * (mean_change + 0.9 * momentum_out)
    weight_list = []
    first_list = []
    second_list = []
    for copy_index in range(N_REPLICA):
        weight_now = weights[copy_index]
        moment_one = first_moment[copy_index]
        moment_two = second_moment[copy_index]
        for inner in range(STEPS):
            batch_rows = inputs[copy_index, inner]
            prediction = jnp.dot(batch_rows, weight_now.astype(jnp.bfloat16), preferred_element_type=jnp.float32) * inv_root
            residual = (prediction - targets[copy_index, inner].astype(jnp.float32)).astype(jnp.bfloat16)
            gradient = lax.dot_general(batch_rows, residual, (((0,), (0,)), ((), ())), preferred_element_type=jnp.float32) * inv_root
            moment_one = 0.9 * moment_one + 0.1 * gradient
            moment_two = 0.95 * moment_two + 0.05 * gradient * gradient
            weight_now = weight_now - 0.05 * (moment_one / (jnp.sqrt(moment_two) + 1e-08) + 0.1 * weight_now)
            weight_now = jnp.where(sync_step[0] == inner, 0.5 * weight_now + 0.5 * global_out, weight_now)
        weight_list.append(weight_now)
        first_list.append(moment_one)
        second_list.append(moment_two)
    return (jnp.stack(weight_list), jnp.stack(first_list), jnp.stack(second_list), global_out, momentum_out)
```

```python
import functools
import math

import jax
import jax.numpy as jnp
from jax import lax
from jax.experimental import pallas as pl
from jax.experimental.pallas import tpu as pltpu
from jax.sharding import PartitionSpec as P

D = 4096
KVW = 512
STEPS = 2
NX, NY, NZ = 4, 4, 2
LOCAL = 1024
TOK = 2 * LOCAL
COLS = KVW // 2
ROWS = 128
HALF = ROWS // 2
CH = COLS // 2
MESH = pl.DeviceIdType.MESH
F32 = jnp.float32
BF16 = jnp.bfloat16

GROUPS = (
    (((0, 2), (1, 2), (2, 2), (3, 2)), (0, 2)),
    (((2, 0), (2, 1), (2, 3)), (1, 2)),
    (((0, 1), (1, 1), (3, 1)), (0, 1)),
    (((1, 0), (1, 3)), (1, 1)),
    (((0, 3), (3, 3)), (0, 3)),
    (((3, 0),), (1, 3)),
    (((0, 0),), None),
)


def dot(a, b):
    return lax.dot_general(a, b, (((1,), (0,)), ((), ())), preferred_element_type=F32)


def kernel(
    x_in,
    t_in,
    w_in,
    m_in,
    v_in,
    gw_in,
    om_in,
    og_in,
    sync_in,
    w_out,
    m_out,
    v_out,
    g_out,
    mo_out,
    xv,
    tv,
    wv,
    mv,
    vv,
    gv,
    gl,
    og,
    wg,
    rt,
    gb,
    r2,
    s1,
    r1,
    loc_sem,
    pre_send,
    pre_recv,
    x_loc,
    x_send,
    x_recv,
    a1_send,
    a1_recv,
    a2_send,
    a2_recv,
    r2_send,
    r2_recv,
    r1_send,
    r1_recv,
    out_loc,
    out_send,
    out_recv,
):
    inv_root = 1.0 / math.sqrt(D)
    rep = lax.axis_index("replica")
    me = lax.axis_index("fsdp")
    c = lax.rem(me, 2)
    zh = lax.rem(lax.div(me, 2), 2)
    y = lax.rem(lax.div(me, 4), 4)
    x = lax.div(me, 16)

    def dev(dx, dy, dz):
        nx, ny = lax.rem(x + dx, 4), lax.rem(y + dy, 4)
        nz = 1 - zh if dz else zh
        return (rep, ((nx * 4 + ny) * 2 + nz) * 2 + c)

    sibling = (rep, me + 1 - 2 * c)
    partner = (1 - rep, me)
    cols = pl.ds(pl.multiple_of(c * COLS, COLS), COLS)
    cols_o = pl.ds(pl.multiple_of((1 - c) * COLS, COLS), COLS)
    rows = pl.ds(pl.multiple_of(c * HALF, HALF), HALF)
    rows_o = pl.ds(pl.multiple_of((1 - c) * HALF, HALF), HALF)

    def remote(src, dst, send, recv, where):
        return pltpu.make_async_remote_copy(
            src_ref=src, dst_ref=dst, send_sem=send, recv_sem=recv, device_id=where, device_id_type=MESH
        )

    local = [
        pltpu.make_async_copy(w_in.at[0, :, cols], wv.at[rows], loc_sem.at[0]),
        pltpu.make_async_copy(m_in.at[0, :, cols], mv.at[rows], loc_sem.at[1]),
        pltpu.make_async_copy(v_in.at[0, :, cols], vv.at[rows], loc_sem.at[2]),
        pltpu.make_async_copy(gw_in, gl.at[0], loc_sem.at[3]),
        pltpu.make_async_copy(om_in, gl.at[1], loc_sem.at[4]),
        pltpu.make_async_copy(og_in.at[0], og.at[0], loc_sem.at[5]),
    ]
    for copy in local:
        copy.start()

    barrier = pltpu.get_barrier_semaphore()
    peers = [(dx, 0, dz) for dx in range(4) for dz in range(2) if dx or dz]
    peers += [(0, dy, dz) for dy in range(1, 4) for dz in range(2)]
    partners = [dev(*p) for p in peers] + [sibling, partner]
    for where in partners:
        pl.semaphore_signal(barrier, inc=1, device_id=where, device_id_type=MESH)
    pl.semaphore_wait(barrier, len(partners))

    pre = [
        remote(w_in.at[0, :, cols_o], wv.at[rows], pre_send.at[0], pre_recv.at[0], sibling),
        remote(m_in.at[0, :, cols_o], mv.at[rows], pre_send.at[1], pre_recv.at[1], sibling),
        remote(v_in.at[0, :, cols_o], vv.at[rows], pre_send.at[2], pre_recv.at[2], sibling),
        remote(og_in.at[0], og.at[1], pre_send.at[3], pre_recv.at[3], partner),
    ]
    for copy in pre:
        copy.start()

    def x_copies(step):
        own = pl.ds(0, LOCAL)
        other = pl.ds(LOCAL, LOCAL)
        return [
            pltpu.make_async_copy(x_in.at[0, step], xv.at[step, own], x_loc.at[step, 0]),
            pltpu.make_async_copy(t_in.at[0, step, :, cols], tv.at[step, own], x_loc.at[step, 1]),
            remote(x_in.at[0, step], xv.at[step, other], x_send.at[step, 0], x_recv.at[step, 0], sibling),
            remote(t_in.at[0, step, :, cols_o], tv.at[step, other], x_send.at[step, 1], x_recv.at[step, 1], sibling),
        ]

    for copy in x_copies(0):
        copy.start()
    local[0].wait()
    pre[0].wait_recv()

    def own_rows(kind):
        return slice(0, HALF) if kind == 0 else slice(HALF, ROWS)

    def delta(kind, along, dz):
        return (along, 0, dz) if kind == 0 else (0, along, dz)

    def long_delta(kind, along):
        return (0, along, 0) if kind == 0 else (along, 0, 0)

    def slot(along, dz):
        return dz * 4 + along

    def back(along):
        return (4 - along) % 4

    def gather_one(kind, along, dz):
        piece = wg.at[x, y, zh, own_rows(kind)]
        return remote(
            piece,
            piece,
            a1_send.at[kind, slot(along, dz)],
            a1_recv.at[kind, slot(back(along), dz)],
            dev(*delta(kind, along, dz)),
        )

    def gather_two(kind, plane, along):
        nz = 1 - zh if plane else zh
        lane = wg.at[:, y, nz, own_rows(kind)] if kind == 0 else wg.at[x, :, nz, own_rows(kind)]
        return remote(
            lane,
            lane,
            a2_send.at[kind, plane, along],
            a2_recv.at[kind, plane, back(along)],
            dev(*long_delta(kind, along)),
        )

    def arrived(copy_of, *args):
        copy_of(*args).wait_recv()

    def scatter_two(kind, along):
        if kind == 0:
            src = gb.at[:, lax.rem(y + along, 4), :, 0:CH]
        else:
            src = gb.at[lax.rem(x + along, 4), :, :, CH:COLS]
        return remote(
            src,
            r2.at[kind, back(along) - 1],
            r2_send.at[kind, along],
            r2_recv.at[kind, back(along)],
            dev(*long_delta(kind, along)),
        )

    def scatter_one(kind, along, dz):
        return remote(
            s1.at[kind, slot(along, dz)],
            r1.at[kind, slot(back(along), dz)],
            r1_send.at[kind, slot(along, dz)],
            r1_recv.at[kind, slot(back(along), dz)],
            dev(*delta(kind, along, dz)),
        )

    short = [(along, dz) for dz in range(2) for along in (2, 1, 3, 0) if along or dz]

    def inner(step, carry):
        wg[x, y, zh] = wv[...].astype(BF16)
        for along, dz in short:
            for kind in range(2):
                gather_one(kind, along, dz).start()

        @pl.when(step == 0)
        def outer():
            for copy in local[1:]:
                copy.wait()
            for copy in pre[1:]:
                copy.wait_recv()
            mean = (og[0].astype(F32) + og[1].astype(F32)) / 2.0
            momentum = 0.9 * gl[1] + mean
            gl[1] = momentum
            gl[0] = gl[0] - 0.7 * (mean + 0.9 * momentum)
            here = pltpu.make_async_copy(gl.at[0, :, cols], gv.at[rows], loc_sem.at[6])
            there = remote(gl.at[0, :, cols_o], gv.at[rows], pre_send.at[4], pre_recv.at[4], sibling)
            outs = [
                pltpu.make_async_copy(gl.at[0], g_out, out_loc.at[3]),
                pltpu.make_async_copy(gl.at[1], mo_out, out_loc.at[4]),
            ]
            for copy in [here, there] + outs:
                copy.start()
            here.wait()
            there.wait()
            for copy in outs:
                copy.wait()
            for copy in pre:
                copy.wait_send()

        for plane in range(2):
            for kind in range(2):
                for along, dz in short:
                    if dz == plane:
                        arrived(gather_one, kind, along, dz)
                for along in (2, 1, 3):
                    gather_two(kind, plane, along).start()
        for kind in range(2):
            for plane in range(2):
                for along in (2, 1, 3):
                    arrived(gather_two, kind, plane, along)
        for copy in x_copies(step):
            copy.wait()

        @pl.when(step == 0)
        def more():
            for copy in x_copies(1):
                copy.start()

        def forward(i, carry):
            block = pl.ds(pl.multiple_of(i * 512, 512), 512)
            product = dot(xv[step, block, :], wg[...].reshape(D, COLS))
            residual = product * inv_root - tv[step, block, :].astype(F32)
            rt[:, block] = residual.astype(BF16).T
            return carry

        lax.fori_loop(0, TOK // 512, forward, 0)

        for kind in range(2):
            for along, dz in short:
                gather_one(kind, along, dz).wait_send()
            for plane in range(2):
                for along in (2, 1, 3):
                    gather_two(kind, plane, along).wait_send()

        for tiles, send in GROUPS:
            for dx, dy in tiles:
                nx, ny = lax.rem(x + dx, 4), lax.rem(y + dy, 4)
                lanes = pl.ds(pl.multiple_of((nx * 4 + ny) * 256, 256), 256)
                tile = dot(rt[...], xv[step, :, lanes]).astype(BF16)
                gb[nx, ny, 0] = tile[:, :ROWS]
                gb[nx, ny, 1] = tile[:, ROWS:]
            if send is not None:
                scatter_two(*send).start()

        for kind in range(2):
            for along in (2, 1, 3):
                arrived(scatter_two, kind, along)
            mine = slice(0, CH) if kind == 0 else slice(CH, COLS)
            for along, dz in [(0, 0)] + short:
                nz = 1 - zh if dz else zh
                far = lax.rem((x if kind == 0 else y) + along, 4)
                here = gb[far, y, nz, mine] if kind == 0 else gb[x, far, nz, mine]
                total = here.astype(F32)
                for source in range(3):
                    total += r2[kind, source, far, nz].astype(F32)
                if along or dz:
                    s1[kind, slot(along, dz)] = total.astype(BF16)
                    scatter_one(kind, along, dz).start()
                else:
                    keep = total
            if kind == 0:
                keep_a = keep
            else:
                keep_b = keep

        halves = []
        for kind, total in ((0, keep_a), (1, keep_b)):
            for along, dz in short:
                arrived(scatter_one, kind, along, dz)
                total += r1[kind, slot(back(along), dz)].astype(F32)
            halves.append(total)
        gradient = jnp.concatenate(halves, axis=0).T * inv_root
        first = 0.9 * mv[...] + 0.1 * gradient
        second = 0.95 * vv[...] + 0.05 * gradient * gradient
        weight = wv[...]
        weight = weight - 0.05 * (first / (jnp.sqrt(second) + 1e-08) + 0.1 * weight)
        weight = jnp.where(sync_in[0] == step, 0.5 * weight + 0.5 * gv[...], weight)
        mv[...] = first
        vv[...] = second
        wv[...] = weight

        for kind in range(2):
            for along in (2, 1, 3):
                scatter_two(kind, along).wait_send()
            for along, dz in short:
                scatter_one(kind, along, dz).wait_send()
        return carry

    lax.fori_loop(0, STEPS, inner, 0)

    ends = []
    for i, (value, out) in enumerate(((wv, w_out), (mv, m_out), (vv, v_out))):
        ends.append(remote(value.at[rows_o], out.at[0, :, cols], out_send.at[i], out_recv.at[i], sibling))
        ends.append(pltpu.make_async_copy(value.at[rows], out.at[0, :, cols], out_loc.at[i]))
    for copy in ends:
        copy.start()
    for copy in ends:
        copy.wait()


def per_device(*args):
    shapes = ((1, 64, KVW),) * 3 + ((64, KVW),) * 2
    dma = pltpu.SemaphoreType.DMA
    anywhere = pl.BlockSpec(memory_space=pl.ANY)
    return pl.pallas_call(
        kernel,
        out_shape=tuple(jax.ShapeDtypeStruct(s, F32) for s in shapes),
        in_specs=[anywhere] * 8 + [pl.BlockSpec(memory_space=pltpu.SMEM)],
        out_specs=(anywhere,) * 5,
        scratch_shapes=[
            pltpu.VMEM((STEPS, TOK, D), BF16),
            pltpu.VMEM((STEPS, TOK, COLS), BF16),
            pltpu.VMEM((ROWS, COLS), F32),
            pltpu.VMEM((ROWS, COLS), F32),
            pltpu.VMEM((ROWS, COLS), F32),
            pltpu.VMEM((ROWS, COLS), F32),
            pltpu.VMEM((2, HALF, KVW), F32),
            pltpu.VMEM((2, HALF, KVW), BF16),
            pltpu.VMEM((NX, NY, NZ, ROWS, COLS), BF16),
            pltpu.VMEM((COLS, TOK), BF16),
            pltpu.VMEM((NX, NY, NZ, COLS, ROWS), BF16),
            pltpu.VMEM((2, 3, 4, NZ, CH, ROWS), BF16),
            pltpu.VMEM((2, 8, CH, ROWS), BF16),
            pltpu.VMEM((2, 8, CH, ROWS), BF16),
            dma((7,)),
            dma((5,)),
            dma((5,)),
            dma((STEPS, 2)),
            dma((STEPS, 2)),
            dma((STEPS, 2)),
            dma((2, 8)),
            dma((2, 8)),
            dma((2, 2, 4)),
            dma((2, 2, 4)),
            dma((2, 4)),
            dma((2, 4)),
            dma((2, 8)),
            dma((2, 8)),
            dma((5,)),
            dma((3,)),
            dma((3,)),
        ],
        compiler_params=pltpu.CompilerParams(
            collective_id=0, has_side_effects=True, vmem_limit_bytes=60 * 1024 * 1024
        ),
    )(*args)


def solution(mesh):
    in_specs = (
        P("replica", None, "fsdp", None),
        P("replica", None, "fsdp", None),
        P("replica", "fsdp", None),
        P("replica", "fsdp", None),
        P("replica", "fsdp", None),
        P("fsdp", None),
        P("fsdp", None),
        P("replica", "fsdp", None),
        P(),
    )
    out_specs = (
        P("replica", "fsdp", None),
        P("replica", "fsdp", None),
        P("replica", "fsdp", None),
        P("fsdp", None),
        P("fsdp", None),
    )
    return jax.shard_map(
        per_device, mesh=mesh, in_specs=in_specs, out_specs=out_specs, check_vma=False
    )
```

```python
import functools
import math

import jax
import jax.numpy as jnp
from jax import lax
from jax.experimental import pallas as pl
from jax.experimental.pallas import tpu as pltpu
from jax.sharding import PartitionSpec as P

D = 4096
KVW = 512
STEPS = 2
NX, NY, NZ = 4, 4, 2
LOCAL = 1024
TOK = 2 * LOCAL
COLS = KVW // 2
ROWS = 128
HALF = ROWS // 2
CHUNKS = 2
CK = COLS // CHUNKS
CH = CK // 2
MESH = pl.DeviceIdType.MESH
F32 = jnp.float32
BF16 = jnp.bfloat16

GROUPS = (
    (((0, 2), (1, 2), (2, 2), (3, 2)), (0, 2)),
    (((2, 0), (2, 1), (2, 3)), (1, 2)),
    (((0, 1), (1, 1), (3, 1)), (0, 1)),
    (((1, 0), (1, 3)), (1, 1)),
    (((0, 3), (3, 3)), (0, 3)),
    (((3, 0),), (1, 3)),
    (((0, 0),), None),
)


def dot(a, b):
    return lax.dot_general(a, b, (((1,), (0,)), ((), ())), preferred_element_type=F32)


def kernel(
    x_in,
    t_in,
    w_in,
    m_in,
    v_in,
    gw_in,
    om_in,
    og_in,
    sync_in,
    w_out,
    m_out,
    v_out,
    g_out,
    mo_out,
    xv,
    tv,
    wv,
    mv,
    vv,
    gv,
    gl,
    og,
    wg,
    rt,
    gb,
    r2,
    s1,
    r1,
    kept,
    loc_sem,
    pre_send,
    pre_recv,
    x_loc,
    x_send,
    x_recv,
    a1_send,
    a1_recv,
    a2_send,
    a2_recv,
    r2_send,
    r2_recv,
    r1_send,
    r1_recv,
    out_loc,
    out_send,
    out_recv,
):
    inv_root = 1.0 / math.sqrt(D)
    rep = lax.axis_index("replica")
    me = lax.axis_index("fsdp")
    c = lax.rem(me, 2)
    zh = lax.rem(lax.div(me, 2), 2)
    y = lax.rem(lax.div(me, 4), 4)
    x = lax.div(me, 16)

    def dev(dx, dy, dz):
        nx, ny = lax.rem(x + dx, 4), lax.rem(y + dy, 4)
        nz = 1 - zh if dz else zh
        return (rep, ((nx * 4 + ny) * 2 + nz) * 2 + c)

    sibling = (rep, me + 1 - 2 * c)
    partner = (1 - rep, me)
    cols = pl.ds(pl.multiple_of(c * COLS, COLS), COLS)
    cols_o = pl.ds(pl.multiple_of((1 - c) * COLS, COLS), COLS)
    rows = pl.ds(pl.multiple_of(c * HALF, HALF), HALF)
    rows_o = pl.ds(pl.multiple_of((1 - c) * HALF, HALF), HALF)

    def remote(src, dst, send, recv, where):
        return pltpu.make_async_remote_copy(
            src_ref=src, dst_ref=dst, send_sem=send, recv_sem=recv, device_id=where, device_id_type=MESH
        )

    local = [
        pltpu.make_async_copy(w_in.at[0, :, cols], wv.at[rows], loc_sem.at[0]),
        pltpu.make_async_copy(m_in.at[0, :, cols], mv.at[rows], loc_sem.at[1]),
        pltpu.make_async_copy(v_in.at[0, :, cols], vv.at[rows], loc_sem.at[2]),
        pltpu.make_async_copy(gw_in, gl.at[0], loc_sem.at[3]),
        pltpu.make_async_copy(om_in, gl.at[1], loc_sem.at[4]),
        pltpu.make_async_copy(og_in.at[0], og.at[0], loc_sem.at[5]),
    ]
    for copy in local:
        copy.start()

    barrier = pltpu.get_barrier_semaphore()
    peers = [(dx, 0, dz) for dx in range(4) for dz in range(2) if dx or dz]
    peers += [(0, dy, dz) for dy in range(1, 4) for dz in range(2)]
    partners = [dev(*p) for p in peers] + [sibling, partner]
    for where in partners:
        pl.semaphore_signal(barrier, inc=1, device_id=where, device_id_type=MESH)
    pl.semaphore_wait(barrier, len(partners))

    pre = [
        remote(w_in.at[0, :, cols_o], wv.at[rows], pre_send.at[0], pre_recv.at[0], sibling),
        remote(m_in.at[0, :, cols_o], mv.at[rows], pre_send.at[1], pre_recv.at[1], sibling),
        remote(v_in.at[0, :, cols_o], vv.at[rows], pre_send.at[2], pre_recv.at[2], sibling),
        remote(og_in.at[0], og.at[1], pre_send.at[3], pre_recv.at[3], partner),
    ]
    for copy in pre:
        copy.start()

    def x_copies(step):
        own = pl.ds(0, LOCAL)
        other = pl.ds(LOCAL, LOCAL)
        return [
            pltpu.make_async_copy(x_in.at[0, step], xv.at[step, own], x_loc.at[step, 0]),
            pltpu.make_async_copy(t_in.at[0, step, :, cols], tv.at[step, own], x_loc.at[step, 1]),
            remote(x_in.at[0, step], xv.at[step, other], x_send.at[step, 0], x_recv.at[step, 0], sibling),
            remote(t_in.at[0, step, :, cols_o], tv.at[step, other], x_send.at[step, 1], x_recv.at[step, 1], sibling),
        ]

    for copy in x_copies(0):
        copy.start()
    local[0].wait()
    pre[0].wait_recv()

    def own_rows(kind):
        return slice(0, HALF) if kind == 0 else slice(HALF, ROWS)

    def delta(kind, along, dz):
        return (along, 0, dz) if kind == 0 else (0, along, dz)

    def long_delta(kind, along):
        return (0, along, 0) if kind == 0 else (along, 0, 0)

    def slot(along, dz):
        return dz * 4 + along

    def back(along):
        return (4 - along) % 4

    def gather_one(k, kind, along, dz):
        piece = wg.at[k, x, y, zh, own_rows(kind)]
        return remote(
            piece,
            piece,
            a1_send.at[k, kind, slot(along, dz)],
            a1_recv.at[k, kind, slot(back(along), dz)],
            dev(*delta(kind, along, dz)),
        )

    def gather_two(k, kind, plane, along):
        nz = 1 - zh if plane else zh
        lane = wg.at[k, :, y, nz, own_rows(kind)] if kind == 0 else wg.at[k, x, :, nz, own_rows(kind)]
        return remote(
            lane,
            lane,
            a2_send.at[k, kind, plane, along],
            a2_recv.at[k, kind, plane, back(along)],
            dev(*long_delta(kind, along)),
        )

    def scatter_two(k, kind, along):
        if kind == 0:
            src = gb.at[k, :, lax.rem(y + along, 4), :, 0:CH]
        else:
            src = gb.at[k, lax.rem(x + along, 4), :, :, CH:CK]
        return remote(
            src,
            r2.at[k, kind, back(along) - 1],
            r2_send.at[k, kind, along],
            r2_recv.at[k, kind, back(along)],
            dev(*long_delta(kind, along)),
        )

    def scatter_one(k, kind, along, dz):
        return remote(
            s1.at[k, kind, slot(along, dz)],
            r1.at[k, kind, slot(back(along), dz)],
            r1_send.at[k, kind, slot(along, dz)],
            r1_recv.at[k, kind, slot(back(along), dz)],
            dev(*delta(kind, along, dz)),
        )

    longs = (2, 1, 3)
    short = [(along, dz) for dz in range(2) for along in (2, 1, 3, 0) if along or dz]

    def gather_start(k):
        wg[k, x, y, zh] = wv[:, k * CK : (k + 1) * CK].astype(BF16)
        for along, dz in short:
            for kind in range(2):
                gather_one(k, kind, along, dz).start()

    def gather_forward(k, plane):
        for kind in range(2):
            for along, dz in short:
                if dz == plane:
                    gather_one(k, kind, along, dz).wait_recv()
            for along in longs:
                gather_two(k, kind, plane, along).start()

    def gather_end(k):
        for plane in range(2):
            for kind in range(2):
                for along in longs:
                    gather_two(k, kind, plane, along).wait_recv()

    def gather_drain(k):
        for kind in range(2):
            for along, dz in short:
                gather_one(k, kind, along, dz).wait_send()
            for plane in range(2):
                for along in longs:
                    gather_two(k, kind, plane, along).wait_send()

    def outer():
        for copy in local[1:]:
            copy.wait()
        for copy in pre[1:]:
            copy.wait_recv()
        mean = (og[0].astype(F32) + og[1].astype(F32)) / 2.0
        momentum = 0.9 * gl[1] + mean
        gl[1] = momentum
        gl[0] = gl[0] - 0.7 * (mean + 0.9 * momentum)
        here = pltpu.make_async_copy(gl.at[0, :, cols], gv.at[rows], loc_sem.at[6])
        there = remote(gl.at[0, :, cols_o], gv.at[rows], pre_send.at[4], pre_recv.at[4], sibling)
        outs = [
            pltpu.make_async_copy(gl.at[0], g_out, out_loc.at[0]),
            pltpu.make_async_copy(gl.at[1], mo_out, out_loc.at[1]),
        ]
        for copy in [here, there] + outs:
            copy.start()
        here.wait()
        there.wait()
        for copy in outs:
            copy.wait()
        for copy in pre:
            copy.wait_send()

    def forward(k, step, first, last):
        def block_of(i, carry):
            block = pl.ds(pl.multiple_of(i * 512, 512), 512)
            product = dot(xv[step, block, :], wg[k].reshape(D, CK))
            residual = product * inv_root - tv[step, block, k * CK : (k + 1) * CK].astype(F32)
            rt[:, block] = residual.astype(BF16).T
            return carry

        lax.fori_loop(first, last, block_of, 0)

    def backward(k, step):
        for tiles, send in GROUPS:
            for dx, dy in tiles:
                nx, ny = lax.rem(x + dx, 4), lax.rem(y + dy, 4)
                lanes = pl.ds(pl.multiple_of((nx * 4 + ny) * 256, 256), 256)
                tile = dot(rt[...], xv[step, :, lanes]).astype(BF16)
                gb[k, nx, ny, 0] = tile[:, :ROWS]
                gb[k, nx, ny, 1] = tile[:, ROWS:]
            if send is not None:
                scatter_two(k, *send).start()

    def add_long(k):
        for kind in range(2):
            for along in longs:
                scatter_two(k, kind, along).wait_recv()
            mine = slice(0, CH) if kind == 0 else slice(CH, CK)
            for along, dz in short + [(0, 0)]:
                nz = 1 - zh if dz else zh
                far = lax.rem((x if kind == 0 else y) + along, 4)
                here = gb[k, far, y, nz, mine] if kind == 0 else gb[k, x, far, nz, mine]
                total = here.astype(F32)
                for source in range(3):
                    total += r2[k, kind, source, far, nz].astype(F32)
                if along or dz:
                    s1[k, kind, slot(along, dz)] = total.astype(BF16)
                    scatter_one(k, kind, along, dz).start()
                else:
                    kept[k, kind] = total

    def update(k, step):
        halves = []
        for kind in range(2):
            total = kept[k, kind]
            for along, dz in short:
                scatter_one(k, kind, along, dz).wait_recv()
                total += r1[k, kind, slot(back(along), dz)].astype(F32)
            halves.append(total)
        gradient = jnp.concatenate(halves, axis=0).T * inv_root
        part = slice(k * CK, (k + 1) * CK)
        first = 0.9 * mv[:, part] + 0.1 * gradient
        second = 0.95 * vv[:, part] + 0.05 * gradient * gradient
        weight = wv[:, part]
        weight = weight - 0.05 * (first / (jnp.sqrt(second) + 1e-08) + 0.1 * weight)
        weight = jnp.where(sync_in[0] == step, 0.5 * weight + 0.5 * gv[:, part], weight)
        mv[:, part] = first
        vv[:, part] = second
        wv[:, part] = weight

    def scatter_drain(k):
        for kind in range(2):
            for along in longs:
                scatter_two(k, kind, along).wait_send()
            for along, dz in short:
                scatter_one(k, kind, along, dz).wait_send()

    def results(k):
        ends = []
        part = pl.ds(pl.multiple_of(c * COLS + k * CK, CK), CK)
        for i, (value, out) in enumerate(((wv, w_out), (mv, m_out), (vv, v_out))):
            mine = pl.ds(k * CK, CK)
            ends.append(
                remote(value.at[rows_o, mine], out.at[0, :, part], out_send.at[k, i], out_recv.at[k, i], sibling)
            )
            ends.append(pltpu.make_async_copy(value.at[rows, mine], out.at[0, :, part], out_loc.at[2 + 3 * k + i]))
        return ends

    gather_start(0)

    def inner(step, carry):
        gather_forward(0, 0)
        gather_forward(0, 1)

        @pl.when(step > 0)
        def late():
            update(1, step - 1)

        gather_start(1)

        @pl.when(step > 0)
        def clear():
            scatter_drain(1)

        gather_forward(1, 0)

        @pl.when(step == 0)
        def once():
            outer()

        gather_end(0)
        for copy in x_copies(step):
            copy.wait()

        @pl.when(step == 0)
        def more():
            for copy in x_copies(1):
                copy.start()

        forward(0, step, 0, 2)
        gather_forward(1, 1)
        forward(0, step, 2, 4)
        gather_drain(0)
        backward(0, step)
        gather_end(1)
        forward(1, step, 0, 4)
        gather_drain(1)
        backward(1, step)
        add_long(0)
        update(0, step)

        @pl.when(step < STEPS - 1)
        def again():
            gather_start(0)

        scatter_drain(0)
        add_long(1)
        return carry

    lax.fori_loop(0, STEPS, inner, 0)

    early = results(0)
    for copy in early:
        copy.start()
    update(1, STEPS - 1)
    ends = results(1)
    for copy in ends:
        copy.start()
    scatter_drain(1)
    for copy in early + ends:
        copy.wait()


def settle(*refs):
    ins, outs, sems = refs[:5], refs[5:10], refs[10]
    copies = [pltpu.make_async_copy(a, b, sems.at[i]) for i, (a, b) in enumerate(zip(ins, outs))]
    for copy in copies:
        copy.start()
    for copy in copies:
        copy.wait()


def per_device(*args):
    shapes = ((1, 64, KVW),) * 3 + ((64, KVW),) * 2
    dma = pltpu.SemaphoreType.DMA
    anywhere = pl.BlockSpec(memory_space=pl.ANY)
    out_shape = tuple(jax.ShapeDtypeStruct(s, F32) for s in shapes)
    values = pl.pallas_call(
        kernel,
        out_shape=out_shape,
        in_specs=[anywhere] * 8 + [pl.BlockSpec(memory_space=pltpu.SMEM)],
        out_specs=(anywhere,) * 5,
        scratch_shapes=[
            pltpu.VMEM((STEPS, TOK, D), BF16),
            pltpu.VMEM((STEPS, TOK, COLS), BF16),
            pltpu.VMEM((ROWS, COLS), F32),
            pltpu.VMEM((ROWS, COLS), F32),
            pltpu.VMEM((ROWS, COLS), F32),
            pltpu.VMEM((ROWS, COLS), F32),
            pltpu.VMEM((2, HALF, KVW), F32),
            pltpu.VMEM((2, HALF, KVW), BF16),
            pltpu.VMEM((CHUNKS, NX, NY, NZ, ROWS, CK), BF16),
            pltpu.VMEM((CK, TOK), BF16),
            pltpu.VMEM((CHUNKS, NX, NY, NZ, CK, ROWS), BF16),
            pltpu.VMEM((CHUNKS, 2, 3, 4, NZ, CH, ROWS), BF16),
            pltpu.VMEM((CHUNKS, 2, 8, CH, ROWS), BF16),
            pltpu.VMEM((CHUNKS, 2, 8, CH, ROWS), BF16),
            pltpu.VMEM((CHUNKS, 2, CH, ROWS), F32),
            dma((7,)),
            dma((5,)),
            dma((5,)),
            dma((STEPS, 2)),
            dma((STEPS, 2)),
            dma((STEPS, 2)),
            dma((CHUNKS, 2, 8)),
            dma((CHUNKS, 2, 8)),
            dma((CHUNKS, 2, 2, 4)),
            dma((CHUNKS, 2, 2, 4)),
            dma((CHUNKS, 2, 4)),
            dma((CHUNKS, 2, 4)),
            dma((CHUNKS, 2, 8)),
            dma((CHUNKS, 2, 8)),
            dma((2 + 3 * CHUNKS,)),
            dma((CHUNKS, 3)),
            dma((CHUNKS, 3)),
        ],
        compiler_params=pltpu.CompilerParams(
            collective_id=0, has_side_effects=True, vmem_limit_bytes=60 * 1024 * 1024
        ),
    )(*args)
    return pl.pallas_call(
        settle,
        out_shape=out_shape,
        in_specs=[anywhere] * 5,
        out_specs=(anywhere,) * 5,
        scratch_shapes=[dma((5,))],
    )(*values)


def solution(mesh):
    in_specs = (
        P("replica", None, "fsdp", None),
        P("replica", None, "fsdp", None),
        P("replica", "fsdp", None),
        P("replica", "fsdp", None),
        P("replica", "fsdp", None),
        P("fsdp", None),
        P("fsdp", None),
        P("replica", "fsdp", None),
        P(),
    )
    out_specs = (
        P("replica", "fsdp", None),
        P("replica", "fsdp", None),
        P("replica", "fsdp", None),
        P("fsdp", None),
        P("fsdp", None),
    )
    return jax.shard_map(
        per_device, mesh=mesh, in_specs=in_specs, out_specs=out_specs, check_vma=False
    )
```

```python
import functools
import math

import jax
import jax.numpy as jnp
from jax import lax
from jax.experimental import pallas as pl
from jax.experimental.pallas import tpu as pltpu
from jax.sharding import PartitionSpec as P

D = 4096
KVW = 512
STEPS = 2
NX, NY, NZ = 4, 4, 2
LOCAL = 1024
TOK = 2 * LOCAL
COLS = KVW // 2
ROWS = 128
HALF = ROWS // 2
CH = COLS // 2
MESH = pl.DeviceIdType.MESH
F32 = jnp.float32
BF16 = jnp.bfloat16

TILES = (
    ((2, 1), (2, 2), (2, 3), (1, 2), (3, 2))
    + ((1, 1), (1, 3), (3, 1), (3, 3))
    + ((0, 2), (2, 0), (0, 1), (1, 0), (0, 3), (3, 0), (0, 0))
)


def dot(a, b):
    return lax.dot_general(a, b, (((1,), (0,)), ((), ())), preferred_element_type=F32)


def kernel(
    x_in,
    t_in,
    w_in,
    m_in,
    v_in,
    gw_in,
    om_in,
    og_in,
    sync_in,
    w_out,
    m_out,
    v_out,
    g_out,
    mo_out,
    xv,
    tv,
    wv,
    mv,
    vv,
    gv,
    gl,
    og,
    wg,
    pt,
    rt,
    gb,
    r2,
    s1,
    r1,
    kept,
    loc_sem,
    pre_send,
    pre_recv,
    x_loc,
    x_send,
    x_recv,
    gz_send,
    gz_recv,
    g1_send,
    g1_recv,
    g2_send,
    g2_recv,
    r2_send,
    r2_recv,
    r1_send,
    r1_recv,
    out_loc,
    out_send,
    out_recv,
):
    inv_root = 1.0 / math.sqrt(D)
    rep = lax.axis_index("replica")
    me = lax.axis_index("fsdp")
    c = lax.rem(me, 2)
    zh = lax.rem(lax.div(me, 2), 2)
    y = lax.rem(lax.div(me, 4), 4)
    x = lax.div(me, 16)

    def dev(dx, dy, dz):
        nx, ny = lax.rem(x + dx, 4), lax.rem(y + dy, 4)
        nz = 1 - zh if dz else zh
        return (rep, ((nx * 4 + ny) * 2 + nz) * 2 + c)

    sibling = (rep, me + 1 - 2 * c)
    partner = (1 - rep, me)
    cols = pl.ds(pl.multiple_of(c * COLS, COLS), COLS)
    cols_o = pl.ds(pl.multiple_of((1 - c) * COLS, COLS), COLS)
    rows = pl.ds(pl.multiple_of(c * HALF, HALF), HALF)
    rows_o = pl.ds(pl.multiple_of((1 - c) * HALF, HALF), HALF)

    def remote(src, dst, send, recv, where):
        return pltpu.make_async_remote_copy(
            src_ref=src, dst_ref=dst, send_sem=send, recv_sem=recv, device_id=where, device_id_type=MESH
        )

    local = [
        pltpu.make_async_copy(w_in.at[0, :, cols], wv.at[rows], loc_sem.at[0]),
        pltpu.make_async_copy(m_in.at[0, :, cols], mv.at[rows], loc_sem.at[1]),
        pltpu.make_async_copy(v_in.at[0, :, cols], vv.at[rows], loc_sem.at[2]),
        pltpu.make_async_copy(gw_in, gl.at[0], loc_sem.at[3]),
        pltpu.make_async_copy(om_in, gl.at[1], loc_sem.at[4]),
        pltpu.make_async_copy(og_in.at[0], og.at[0], loc_sem.at[5]),
    ]
    for copy in local:
        copy.start()

    barrier = pltpu.get_barrier_semaphore()
    peers = [(dx, 0, dz) for dx in range(4) for dz in range(2) if dx or dz]
    peers += [(0, dy, dz) for dy in range(1, 4) for dz in range(2)]
    partners = [dev(*p) for p in peers] + [sibling, partner]
    for where in partners:
        pl.semaphore_signal(barrier, inc=1, device_id=where, device_id_type=MESH)
    pl.semaphore_wait(barrier, len(partners))

    pre = [
        remote(w_in.at[0, :, cols_o], wv.at[rows], pre_send.at[0], pre_recv.at[0], sibling),
        remote(m_in.at[0, :, cols_o], mv.at[rows], pre_send.at[1], pre_recv.at[1], sibling),
        remote(v_in.at[0, :, cols_o], vv.at[rows], pre_send.at[2], pre_recv.at[2], sibling),
        remote(og_in.at[0], og.at[1], pre_send.at[3], pre_recv.at[3], partner),
    ]
    for copy in pre:
        copy.start()

    def x_copies(step):
        own = pl.ds(0, LOCAL)
        other = pl.ds(LOCAL, LOCAL)
        return [
            pltpu.make_async_copy(x_in.at[0, step], xv.at[step, own], x_loc.at[step, 0]),
            pltpu.make_async_copy(t_in.at[0, step, :, cols], tv.at[step, own], x_loc.at[step, 1]),
            remote(x_in.at[0, step], xv.at[step, other], x_send.at[step, 0], x_recv.at[step, 0], sibling),
            remote(t_in.at[0, step, :, cols_o], tv.at[step, other], x_send.at[step, 1], x_recv.at[step, 1], sibling),
        ]

    for copy in x_copies(0):
        copy.start()
    local[0].wait()
    pre[0].wait_recv()

    def half(kind):
        return slice(0, HALF) if kind == 0 else slice(HALF, ROWS)

    def long_delta(kind, along):
        return (0, along, 0) if kind == 0 else (along, 0, 0)

    def short_delta(kind, along, dz):
        return (along, 0, dz) if kind == 0 else (0, along, dz)

    def slot(along, dz):
        return dz * 4 + along

    def back(along):
        return (4 - along) % 4

    def plane_z(plane):
        return 1 - zh if plane else zh

    def gather_z():
        piece = wg.at[x, y, zh]
        return remote(piece, piece, gz_send.at[0], gz_recv.at[0], dev(0, 0, 1))

    def gather_ring(plane, axis, along):
        piece = wg.at[x, y, plane_z(plane)]
        return remote(
            piece,
            piece,
            g1_send.at[plane, axis, along],
            g1_recv.at[plane, axis, back(along)],
            dev(*((along, 0, 0) if axis == 0 else (0, along, 0))),
        )

    def gather_long(plane, kind, along, rel):
        nz = plane_z(plane)
        if kind == 0:
            piece = wg.at[lax.rem(x + rel, 4), y, nz, half(0)]
        else:
            piece = wg.at[x, lax.rem(y + rel, 4), nz, half(1)]
        return remote(
            piece,
            piece,
            g2_send.at[plane, kind, along, rel],
            g2_recv.at[plane, kind, back(along), rel],
            dev(*long_delta(kind, along)),
        )

    def scatter_long(kind, along, rel):
        if kind == 0:
            src = gb.at[lax.rem(x + rel, 4), lax.rem(y + along, 4), :, 0:CH]
        else:
            src = gb.at[lax.rem(x + along, 4), lax.rem(y + rel, 4), :, CH:COLS]
        return remote(
            src,
            r2.at[kind, back(along) - 1, rel],
            r2_send.at[kind, along, rel],
            r2_recv.at[kind, back(along), rel],
            dev(*long_delta(kind, along)),
        )

    def scatter_short(kind, along, dz):
        return remote(
            s1.at[kind, slot(along, dz)],
            r1.at[kind, slot(back(along), dz)],
            r1_send.at[kind, slot(along, dz)],
            r1_recv.at[kind, slot(back(along), dz)],
            dev(*short_delta(kind, along, dz)),
        )

    others = (1, 3, 2)
    short = [(along, dz) for dz in range(2) for along in (2, 1, 3, 0) if along or dz]

    def gather_start():
        wg[x, y, zh] = wv[...].astype(BF16)
        gather_z().start()
        for along in others:
            for axis in range(2):
                gather_ring(0, axis, along).start()

    def gather_forward(plane):
        for rel in others:
            for kind in range(2):
                gather_ring(plane, kind, back(rel)).wait_recv()
                for along in others:
                    gather_long(plane, kind, along, rel).start()

    def gather_turn():
        gather_z().wait_recv()
        for along in others:
            for axis in range(2):
                gather_ring(1, axis, along).start()

    def gather_end(plane):
        for kind in range(2):
            for along in others:
                for rel in others:
                    gather_long(plane, kind, along, rel).wait_recv()

    def gather_drain():
        gather_z().wait_send()
        for plane in range(2):
            for kind in range(2):
                for along in others:
                    gather_ring(plane, kind, along).wait_send()
                    for rel in others:
                        gather_long(plane, kind, along, rel).wait_send()

    def outer_ends():
        here = pltpu.make_async_copy(gl.at[0, :, cols], gv.at[rows], loc_sem.at[6])
        there = remote(gl.at[0, :, cols_o], gv.at[rows], pre_send.at[4], pre_recv.at[4], sibling)
        outs = [
            pltpu.make_async_copy(gl.at[0], g_out, out_loc.at[0]),
            pltpu.make_async_copy(gl.at[1], mo_out, out_loc.at[1]),
        ]
        return [here, there] + outs

    def outer():
        for copy in local[1:]:
            copy.wait()
        for copy in pre[1:]:
            copy.wait_recv()
        mean = (og[0].astype(F32) + og[1].astype(F32)) / 2.0
        momentum = 0.9 * gl[1] + mean
        gl[1] = momentum
        gl[0] = gl[0] - 0.7 * (mean + 0.9 * momentum)
        for copy in outer_ends():
            copy.start()

    def forward(plane, step):
        nz = plane_z(plane)

        def block_of(i, carry):
            block = pl.ds(pl.multiple_of(i * 512, 512), 512)
            strips = [
                xv[step, block, pl.ds(pl.multiple_of(k * 256 + nz * ROWS, ROWS), ROWS)] for k in range(NX * NY)
            ]
            part = dot(jnp.concatenate(strips, axis=1), wg[:, :, nz].reshape(NX * NY * ROWS, COLS))
            if plane == 0:
                pt[block, :] = part
            else:
                product = pt[block, :] + part
                residual = product * inv_root - tv[step, block, :].astype(F32)
                rt[:, block] = residual.astype(BF16).T
            return carry

        lax.fori_loop(0, TOK // 512, block_of, 0)

    def backward(step):
        for dx, dy in TILES:
            nx, ny = lax.rem(x + dx, 4), lax.rem(y + dy, 4)
            lanes = pl.ds(pl.multiple_of((nx * 4 + ny) * 256, 256), 256)
            tile = dot(rt[...], xv[step, :, lanes]).astype(BF16)
            gb[nx, ny, 0] = tile[:, :ROWS]
            gb[nx, ny, 1] = tile[:, ROWS:]
            if dy:
                scatter_long(0, dy, dx).start()
            if dx:
                scatter_long(1, dx, dy).start()

    def add_long():
        for rel in (2, 1, 3, 0):
            for kind in range(2):
                for along in others:
                    scatter_long(kind, along, rel).wait_recv()
                mine = slice(0, CH) if kind == 0 else slice(CH, COLS)
                far = lax.rem((x if kind == 0 else y) + rel, 4)
                for dz in (1, 0):
                    nz = plane_z(dz)
                    here = gb[far, y, nz, mine] if kind == 0 else gb[x, far, nz, mine]
                    total = here.astype(F32)
                    for source in range(3):
                        total += r2[kind, source, rel, nz].astype(F32)
                    if rel or dz:
                        s1[kind, slot(rel, dz)] = total.astype(BF16)
                        scatter_short(kind, rel, dz).start()
                    else:
                        kept[kind] = total

    def update(step):
        halves = []
        for kind in range(2):
            total = kept[kind]
            for along, dz in short:
                scatter_short(kind, along, dz).wait_recv()
                total += r1[kind, slot(back(along), dz)].astype(F32)
            halves.append(total)
        gradient = jnp.concatenate(halves, axis=0).T * inv_root
        first = 0.9 * mv[...] + 0.1 * gradient
        second = 0.95 * vv[...] + 0.05 * gradient * gradient
        weight = wv[...]
        weight = weight - 0.05 * (first / (jnp.sqrt(second) + 1e-08) + 0.1 * weight)
        weight = jnp.where(sync_in[0] == step, 0.5 * weight + 0.5 * gv[...], weight)
        mv[...] = first
        vv[...] = second
        wv[...] = weight

    def scatter_drain():
        for kind in range(2):
            for along in others:
                for rel in range(4):
                    scatter_long(kind, along, rel).wait_send()
            for along, dz in short:
                scatter_short(kind, along, dz).wait_send()

    gather_start()

    def inner(step, carry):
        gather_turn()
        gather_forward(0)

        @pl.when(step == 0)
        def once():
            outer()

        gather_forward(1)
        gather_end(0)
        for copy in x_copies(step):
            copy.wait()

        @pl.when(step == 0)
        def more():
            for copy in x_copies(1):
                copy.start()
            for copy in outer_ends():
                copy.wait()
            for copy in pre:
                copy.wait_send()

        forward(0, step)
        gather_end(1)
        forward(1, step)
        gather_drain()
        backward(step)
        add_long()
        update(step)

        @pl.when(step < STEPS - 1)
        def again():
            gather_start()

        scatter_drain()
        return carry

    lax.fori_loop(0, STEPS, inner, 0)

    ends = []
    for i, (value, out) in enumerate(((wv, w_out), (mv, m_out), (vv, v_out))):
        ends.append(remote(value.at[rows_o], out.at[0, :, cols], out_send.at[i], out_recv.at[i], sibling))
        ends.append(pltpu.make_async_copy(value.at[rows], out.at[0, :, cols], out_loc.at[2 + i]))
    for copy in ends:
        copy.start()
    for copy in ends:
        copy.wait()


def settle(*refs):
    ins, outs, sems = refs[:5], refs[5:10], refs[10]
    copies = [pltpu.make_async_copy(a, b, sems.at[i]) for i, (a, b) in enumerate(zip(ins, outs))]
    for copy in copies:
        copy.start()
    for copy in copies:
        copy.wait()


def per_device(*args):
    shapes = ((1, 64, KVW),) * 3 + ((64, KVW),) * 2
    dma = pltpu.SemaphoreType.DMA
    anywhere = pl.BlockSpec(memory_space=pl.ANY)
    out_shape = tuple(jax.ShapeDtypeStruct(s, F32) for s in shapes)
    values = pl.pallas_call(
        kernel,
        out_shape=out_shape,
        in_specs=[anywhere] * 8 + [pl.BlockSpec(memory_space=pltpu.SMEM)],
        out_specs=(anywhere,) * 5,
        scratch_shapes=[
            pltpu.VMEM((STEPS, TOK, D), BF16),
            pltpu.VMEM((STEPS, TOK, COLS), BF16),
            pltpu.VMEM((ROWS, COLS), F32),
            pltpu.VMEM((ROWS, COLS), F32),
            pltpu.VMEM((ROWS, COLS), F32),
            pltpu.VMEM((ROWS, COLS), F32),
            pltpu.VMEM((2, HALF, KVW), F32),
            pltpu.VMEM((2, HALF, KVW), BF16),
            pltpu.VMEM((NX, NY, NZ, ROWS, COLS), BF16),
            pltpu.VMEM((TOK, COLS), F32),
            pltpu.VMEM((COLS, TOK), BF16),
            pltpu.VMEM((NX, NY, NZ, COLS, ROWS), BF16),
            pltpu.VMEM((2, 3, 4, NZ, CH, ROWS), BF16),
            pltpu.VMEM((2, 8, CH, ROWS), BF16),
            pltpu.VMEM((2, 8, CH, ROWS), BF16),
            pltpu.VMEM((2, CH, ROWS), F32),
            dma((7,)),
            dma((5,)),
            dma((5,)),
            dma((STEPS, 2)),
            dma((STEPS, 2)),
            dma((STEPS, 2)),
            dma((1,)),
            dma((1,)),
            dma((2, 2, 4)),
            dma((2, 2, 4)),
            dma((2, 2, 4, 4)),
            dma((2, 2, 4, 4)),
            dma((2, 4, 4)),
            dma((2, 4, 4)),
            dma((2, 8)),
            dma((2, 8)),
            dma((5,)),
            dma((3,)),
            dma((3,)),
        ],
        compiler_params=pltpu.CompilerParams(
            collective_id=0, has_side_effects=True, vmem_limit_bytes=60 * 1024 * 1024
        ),
    )(*args)
    return pl.pallas_call(
        settle,
        out_shape=out_shape,
        in_specs=[anywhere] * 5,
        out_specs=(pl.BlockSpec(memory_space=pltpu.VMEM),) * 5,
        scratch_shapes=[dma((5,))],
    )(*values)


def solution(mesh):
    in_specs = (
        P("replica", None, "fsdp", None),
        P("replica", None, "fsdp", None),
        P("replica", "fsdp", None),
        P("replica", "fsdp", None),
        P("replica", "fsdp", None),
        P("fsdp", None),
        P("fsdp", None),
        P("replica", "fsdp", None),
        P(),
    )
    out_specs = (
        P("replica", "fsdp", None),
        P("replica", "fsdp", None),
        P("replica", "fsdp", None),
        P("fsdp", None),
        P("fsdp", None),
    )
    return jax.shard_map(
        per_device, mesh=mesh, in_specs=in_specs, out_specs=out_specs, check_vma=False
    )
```
